32 devices in a mesh: tiles: 16 (over z, y, x), chan: 2 (over core).
Axes of the slice: x: 2, y: 2, z: 4, core: 2. Of those that a mesh axis runs over, the one named last changes fastest.
Arguments:
- ocean_state: bfloat16 [16, 22, 2, 16, 3072], P('tiles', None, 'chan'), may hold values from -24 to 24
- land_mask: int32 [16, 22], P('tiles'), may hold values from 0 to 1, as said below
- cotangent: bfloat16 [224, 2, 16, 3072], P('tiles', 'chan'), may hold values from -6 to 6
- depth_kernel: float32 [7, 7, 384], P(None, None, 'chan'), may hold values from -1.8 to 1.8
- norm_gain: float32 [384], P('chan'), may hold values from 0.5 to 1.5
- norm_shift: float32 [384], P('chan'), may hold values from -3 to 3
- weight_in: bfloat16 [384, 1536], P(None, 'chan'), may hold values from -0.3125 to 0.3125
- bias_in: float32 [1536], P('chan'), may hold values from -3 to 3
- weight_out: bfloat16 [1536, 384], P('chan'), may hold values from -0.15625 to 0.15625
- bias_out: float32 [384], P('chan'), may hold values from -3 to 3
- layer_scale: float32 [384], P('chan'), may hold values from 0.3 to 1
Outputs:
- block_out: bfloat16 [224, 2, 16, 3072], P('tiles', 'chan')
- grad_state: bfloat16 [16, 22, 2, 16, 3072], P('tiles', None, 'chan')
- grad_kernel: float32 [7, 7, 384], P(None, None, 'chan')
- grad_gain: float32 [384], P('chan')
- grad_shift: float32 [384], P('chan')
- grad_weight_in: float32 [384, 1536], P(None, 'chan')
- grad_bias_in: float32 [1536], P('chan')
- grad_weight_out: float32 [1536, 384], P('chan')
- grad_bias_out: float32 [384], P('chan')
- grad_scale: float32 [384], P('chan')
The draws below stay inside these ranges and needn't reach their ends.
Inputs may be any that keep to these rules, and one draw needn't show every extreme that they name: `land_mask`: exactly 224 entries are 1, and some band is ocean in all its 22 slots.
All inputs are finite; a program needn't handle non-finite values.
Results may differ from the reference program's by a relative error of at most 0.014.
Values may be sent and summed in bfloat16 or wider, within the bound.
A program may use at most 128 MiB of HBM per device.

```python
import math
import jax
import jax.numpy as jnp
from jax import lax

CHANNELS = 384
HALVES = 2
HALF = 192
HIDDEN_UNITS = 1536
KERNEL = 7
TILE_SIDE = 16
TILE_DEV = 14
SLOT_DEV = 22
BANDS = 16
OCEAN = 224
CELLS = 57344
N_CHAN = 2


def draw_land_mask(key, part):
    first_key, second_key, third_key = jax.random.split(jax.random.fold_in(key, 11), 3)
    slot_total = BANDS * SLOT_DEV
    ordering = jax.random.permutation(first_key, slot_total).astype(jnp.int32).reshape(BANDS, SLOT_DEV)
    tiering = jax.random.randint(second_key, (BANDS, 1), 0, 3).astype(jnp.int32)
    full_band = jax.random.randint(third_key, (), 0, BANDS).astype(jnp.int32)
    tiering = jnp.where(jnp.arange(BANDS, dtype=jnp.int32)[:, None] == full_band, 3, tiering)
    scores = (tiering * slot_total + ordering).reshape(-1)
    chosen = lax.top_k(scores, OCEAN)[1]
    flat_mask = jnp.zeros((slot_total,), jnp.int32).at[chosen].set(1)
    return flat_mask.reshape(BANDS, SLOT_DEV)


def draw_ocean_state(key, part):
    first_key, second_key = jax.random.split(jax.random.fold_in(key, 23), 2)
    shape_full = (BANDS, SLOT_DEV, TILE_SIDE, TILE_SIDE, CHANNELS)
    cell_scale = jnp.exp(jax.random.uniform(second_key, shape_full[:4] + (1,), jnp.float32, jnp.log(0.4), jnp.log(4.0)))
    base_values = jnp.clip(jax.random.normal(first_key, shape_full, jnp.float32), -6.0, 6.0)
    cells_values = base_values * cell_scale
    arranged = cells_values.reshape(BANDS, SLOT_DEV, TILE_SIDE, TILE_SIDE, HALVES, HALF).transpose(0, 1, 4, 2, 3, 5)
    return arranged.reshape(BANDS, SLOT_DEV, HALVES, TILE_SIDE, TILE_SIDE * HALF).astype(jnp.bfloat16)


def draw_depth_kernel(key, part):
    first_key, second_key = jax.random.split(jax.random.fold_in(key, 37), 2)
    channel_scale = jnp.exp(jax.random.uniform(second_key, (1, 1, CHANNELS), jnp.float32, jnp.log(0.3), jnp.log(3.0)))
    base_values = jnp.clip(jax.random.normal(first_key, (KERNEL, KERNEL, CHANNELS), jnp.float32), -4.0, 4.0)
    return base_values * channel_scale / KERNEL


def steps_of(rng, shape, shards, smallest, largest):
    factor_of, own = 1.0, jax.random.fold_in(rng, 6)
    for position, blocks in shards:
        draws = jnp.exp(jax.random.uniform(jax.random.fold_in(own, position), (blocks,), jnp.float32, smallest / len(shards), largest / len(shards)))
        factor_of = factor_of * jnp.repeat(draws, shape[position] // blocks).reshape([-1 if axis == position else 1 for axis in range(len(shape))])
    return factor_of


def gaussian(stream_key, extent, width, bound, shards=(), kind=jnp.bfloat16):
    values = width * jax.random.normal(stream_key, extent, jnp.float32)
    if shards:
        values = values * steps_of(stream_key, extent, shards, -0.22, 0.18)
    return jnp.clip(values, -bound, bound).astype(kind)


def setup_inputs(seed: int = 0) -> dict:
    key_list = jax.random.split(jax.random.key(seed), 12)
    ocean_state = draw_ocean_state(jax.random.fold_in(key_list[11], 71), 0)
    land_mask = draw_land_mask(jax.random.fold_in(key_list[11], 71), 0)
    cotangent = gaussian(key_list[2], (OCEAN, HALVES, TILE_SIDE, TILE_SIDE * HALF), 1.0, 6.0, ((0, 16), (1, 2)))
    depth_kernel = draw_depth_kernel(jax.random.fold_in(key_list[11], 71), 0)
    norm_gain = jnp.clip(0.5 + 1.0 * jax.random.uniform(key_list[4], (CHANNELS,), jnp.float32) ** steps_of(key_list[4], (CHANNELS,), ((0, 2),), -0.2, 0.2), 0.5, 1.5)
    norm_shift = gaussian(key_list[5], (CHANNELS,), 0.5, 3.0, ((0, 2),), jnp.float32)
    weight_in = gaussian(key_list[6], (CHANNELS, HIDDEN_UNITS), CHANNELS ** -0.5, 0.3125, ((1, 2),))
    bias_in = gaussian(key_list[7], (HIDDEN_UNITS,), 0.5, 3.0, ((0, 2),), jnp.float32)
    weight_out = gaussian(key_list[8], (HIDDEN_UNITS, CHANNELS), HIDDEN_UNITS ** -0.5, 0.15625, ((0, 2),))
    bias_out = gaussian(key_list[9], (CHANNELS,), 0.5, 3.0, ((0, 2),), jnp.float32)
    layer_scale = jnp.clip(jnp.exp(math.log(1.0) - 1.2039728 * jax.random.uniform(key_list[10], (CHANNELS,), jnp.float32) ** steps_of(key_list[10], (CHANNELS,), ((0, 2),), -0.2, 0.2)), 0.3, 1.0)
    return {"ocean_state": ocean_state, "land_mask": land_mask, "cotangent": cotangent, "depth_kernel": depth_kernel, "norm_gain": norm_gain, "norm_shift": norm_shift, "weight_in": weight_in, "bias_in": bias_in, "weight_out": weight_out, "bias_out": bias_out, "layer_scale": layer_scale}


EPS = 1e-06
ROOT_TWO_PI = 0.7978845608028654
CUBIC = 0.044715

def gelu_pair(values):
    inner_arg = ROOT_TWO_PI * (values + CUBIC * values * values * values)
    tangent = jnp.tanh(inner_arg)
    gelu_value = 0.5 * values * (1.0 + tangent)
    gelu_slope = 0.5 * (1.0 + tangent) + 0.5 * values * (1.0 - tangent * tangent) * ROOT_TWO_PI * (1.0 + 3.0 * CUBIC * values * values)
    return (gelu_value, gelu_slope)

def rounded(values):
    return lax.optimization_barrier(values.astype(jnp.bfloat16)).astype(jnp.float32)

def depthwise(padded, kernel, out_side):
    kernel_span = kernel.shape[0]
    accumulated = jnp.zeros((padded.shape[0], out_side, out_side, padded.shape[3]), jnp.float32)
    for down_step in range(kernel_span):
        for east_step in range(kernel_span):
            window = padded[:, down_step:down_step + out_side, east_step:east_step + out_side, :]
            accumulated = accumulated + window.astype(jnp.float32) * kernel[down_step, east_step]
    return accumulated

def spread_back(back_tiles, kernel, out_side):
    reach_cells = kernel.shape[0] - 1
    widened = jnp.pad(back_tiles, ((0, 0), (reach_cells, reach_cells), (reach_cells, reach_cells), (0, 0)))
    return depthwise(widened, kernel[::-1, ::-1], out_side)

def kernel_grads(back_tiles, framed, tile_side, kernel_span):
    back_float = back_tiles.astype(jnp.float32)
    rows_out = []
    for down_step in range(kernel_span):
        kernel_row = []
        for east_step in range(kernel_span):
            window = framed[:, down_step:down_step + tile_side, east_step:east_step + tile_side, :].astype(jnp.float32)
            kernel_row.append(lax.optimization_barrier(jnp.sum(back_float * window, axis=(0, 1, 2))))
        rows_out.append(jnp.stack(kernel_row))
    return jnp.stack(rows_out)

def tile_pass(window, upstream_tile, depth_kernel, norm_gain, norm_shift, weight_in, bias_in, weight_out, bias_out, layer_scale):
    tile_side = upstream_tile.shape[0]
    channels = upstream_tile.shape[2]
    kernel_span = depth_kernel.shape[0]
    margin = kernel_span // 2
    padded_side = tile_side + 2 * margin
    cell_count = tile_side * tile_side
    framed = window[None]
    mixed_field = depthwise(framed, depth_kernel, tile_side).reshape(cell_count, channels)
    cell_mean = lax.optimization_barrier(jnp.sum(mixed_field, axis=1)) / channels
    variance = lax.optimization_barrier(jnp.sum(mixed_field * mixed_field, axis=1)) / channels - cell_mean * cell_mean
    norm_factor = lax.rsqrt(variance + EPS)
    normed = (mixed_field - cell_mean[:, None]) * norm_factor[:, None]
    features = (normed * norm_gain + norm_shift).astype(jnp.bfloat16)
    hidden = jnp.dot(features, weight_in, preferred_element_type=jnp.float32) + bias_in
    active, active_slope = gelu_pair(hidden)
    active = active.astype(jnp.bfloat16)
    group_size = weight_in.shape[1] // N_CHAN
    branch = jnp.zeros((cell_count, channels), jnp.float32)
    for group_index in range(N_CHAN):
        group_start = group_index * group_size
        branch = branch + rounded(jnp.dot(active[:, group_start:group_start + group_size], weight_out[group_start:group_start + group_size], preferred_element_type=jnp.float32))
    branch = branch + bias_out
    residual = window[margin:margin + tile_side, margin:margin + tile_side].astype(jnp.float32).reshape(cell_count, channels)
    block_tile = (residual + layer_scale * branch).astype(jnp.bfloat16).reshape(tile_side, tile_side, channels)
    upstream = upstream_tile.astype(jnp.float32).reshape(cell_count, channels)
    scaled = layer_scale * upstream
    scaled_bf = scaled.astype(jnp.bfloat16)
    grad_scale = lax.optimization_barrier(jnp.sum(upstream * branch, axis=0))
    grad_bias_out = lax.optimization_barrier(jnp.sum(scaled, axis=0))
    grad_weight_out = jnp.dot(active.T, scaled_bf, preferred_element_type=jnp.float32)
    back_hidden = jnp.dot(scaled_bf, weight_out.T, preferred_element_type=jnp.float32) * active_slope
    back_hidden_bf = back_hidden.astype(jnp.bfloat16)
    grad_weight_in = jnp.dot(features.T, back_hidden_bf, preferred_element_type=jnp.float32)
    grad_bias_in = lax.optimization_barrier(jnp.sum(back_hidden, axis=0))
    back_features = jnp.zeros((cell_count, channels), jnp.float32)
    for group_index in range(N_CHAN):
        group_start = group_index * group_size
        back_features = back_features + rounded(jnp.dot(back_hidden_bf[:, group_start:group_start + group_size], weight_in[:, group_start:group_start + group_size].T, preferred_element_type=jnp.float32))
    back_normed = back_features * norm_gain
    grad_gain = lax.optimization_barrier(jnp.sum(back_features * normed, axis=0))
    grad_shift = lax.optimization_barrier(jnp.sum(back_features, axis=0))
    first_mean = lax.optimization_barrier(jnp.sum(back_normed, axis=1)) / channels
    second_mean = lax.optimization_barrier(jnp.sum(back_normed * normed, axis=1)) / channels
    back_mixed = norm_factor[:, None] * (back_normed - first_mean[:, None] - normed * second_mean[:, None])
    back_tiles = back_mixed.astype(jnp.bfloat16).reshape(1, tile_side, tile_side, channels)
    grad_kernel = kernel_grads(back_tiles, framed, tile_side, kernel_span)
    spread_terms = spread_back(back_tiles, depth_kernel, padded_side)[0].astype(jnp.bfloat16)
    tile_sums = (grad_kernel, grad_gain, grad_shift, grad_weight_in, grad_bias_in, grad_weight_out, grad_bias_out, grad_scale)
    return (block_tile, spread_terms, tile_sums)

def reference(ocean_state, land_mask, cotangent, depth_kernel, norm_gain, norm_shift, weight_in, bias_in, weight_out, bias_out, layer_scale):
    band_count, slot_count = land_mask.shape
    halves = ocean_state.shape[2]
    tile_side = ocean_state.shape[3]
    channels = depth_kernel.shape[2]
    half_chans = channels // halves
    cells_state = ocean_state.reshape(band_count, slot_count, halves, tile_side, tile_side, half_chans).transpose(0, 1, 3, 4, 2, 5).reshape(band_count, slot_count, tile_side, tile_side, channels)
    list_count = cotangent.shape[0]
    cells_cotangent = cotangent.reshape(list_count, halves, tile_side, tile_side, half_chans).transpose(0, 2, 3, 1, 4).reshape(list_count, tile_side, tile_side, channels)
    kernel_span = depth_kernel.shape[0]
    margin = kernel_span // 2
    padded_side = tile_side + 2 * margin
    grid_rows = band_count * tile_side
    grid_cols = slot_count * tile_side
    masked = cells_state * land_mask.astype(jnp.bfloat16)[:, :, None, None, None]
    state_field = masked.transpose(0, 2, 1, 3, 4).reshape(grid_rows, grid_cols, channels)
    state_field = jnp.concatenate([state_field[:, grid_cols - margin:], state_field, state_field[:, :margin]], axis=1)
    state_field = jnp.pad(state_field, ((margin, margin), (0, 0), (0, 0)))
    ocean_ids = jnp.nonzero(land_mask.reshape(-1) > 0, size=OCEAN)[0].astype(jnp.int32)
    zero_sums = (jnp.zeros(depth_kernel.shape, jnp.float32), jnp.zeros((channels,), jnp.float32), jnp.zeros((channels,), jnp.float32), jnp.zeros(weight_in.shape, jnp.float32), jnp.zeros(bias_in.shape, jnp.float32), jnp.zeros(weight_out.shape, jnp.float32), jnp.zeros((channels,), jnp.float32), jnp.zeros((channels,), jnp.float32))
    gradient_field = jnp.zeros((grid_rows + 2 * margin, grid_cols + 2 * margin, channels), jnp.float32)

    def per_tile(carried, list_index):
        totals, gradient_field = carried
        tile_rank = list_index % TILE_DEV * BANDS + list_index // TILE_DEV
        tile_id = ocean_ids[tile_rank]
        start_row = (tile_id // slot_count * tile_side).astype(jnp.int32)
        start_col = (tile_id % slot_count * tile_side).astype(jnp.int32)
        anchor = (start_row, start_col, jnp.zeros((), jnp.int32))
        window = lax.dynamic_slice(state_field, anchor, (padded_side, padded_side, channels))
        upstream_tile = lax.dynamic_index_in_dim(cells_cotangent, list_index, 0, keepdims=False)
        block_tile, spread_terms, tile_sums = tile_pass(window, upstream_tile, depth_kernel, norm_gain, norm_shift, weight_in, bias_in, weight_out, bias_out, layer_scale)
        current = lax.dynamic_slice(gradient_field, anchor, (padded_side, padded_side, channels))
        gradient_field = lax.dynamic_update_slice(gradient_field, current + spread_terms.astype(jnp.float32), anchor)
        totals = tuple((before + update for before, update in zip(totals, tile_sums)))
        return ((totals, gradient_field), block_tile)
    (totals, gradient_field), blocks = lax.scan(per_tile, (zero_sums, gradient_field), jnp.arange(OCEAN, dtype=jnp.int32))
    folded = gradient_field[:, margin:margin + grid_cols]
    folded = folded + jnp.pad(gradient_field[:, margin + grid_cols:], ((0, 0), (0, grid_cols - margin), (0, 0)))
    folded = folded + jnp.pad(gradient_field[:, :margin], ((0, 0), (grid_cols - margin, 0), (0, 0)))
    folded = folded[margin:margin + grid_rows]
    folded = folded.reshape(band_count, tile_side, slot_count, tile_side, channels).transpose(0, 2, 1, 3, 4)
    grad_cells = (folded * land_mask.astype(jnp.float32)[:, :, None, None, None]).astype(jnp.bfloat16)
    grad_state = grad_cells.reshape(band_count, slot_count, tile_side, tile_side, halves, half_chans).transpose(0, 1, 4, 2, 3, 5).reshape(band_count, slot_count, halves, tile_side, tile_side * half_chans)
    blocks_out = blocks.reshape(list_count, tile_side, tile_side, halves, half_chans).transpose(0, 3, 1, 2, 4).reshape(list_count, halves, tile_side, tile_side * half_chans)
    norm_cells = float(CELLS) ** 0.5
    scaled_sums = [summand / norm_cells for summand in totals]
    return (blocks_out, grad_state, scaled_sums[0], scaled_sums[1], scaled_sums[2], scaled_sums[3], scaled_sums[4], scaled_sums[5], scaled_sums[6], scaled_sums[7])
```

```python
import jax
import jax.numpy as jnp
from jax import lax
from jax.sharding import PartitionSpec as P

EPS = 1e-06
ROOT_TWO_PI = 0.7978845608028654
CUBIC = 0.044715
SWAP = ((0, 1), (1, 0))


def swapped(value):
    return lax.ppermute(value, "chan", SWAP)


def row_halo(field, width):
    count = lax.axis_size("tiles")
    forward = [(i, i + 1) for i in range(count - 1)]
    backward = [(target, source) for source, target in forward]
    low = lax.ppermute(field[field.shape[0] - width :], "tiles", forward)
    high = lax.ppermute(field[:width], "tiles", backward)
    return jnp.concatenate([low, field, high], axis=0)


def gelu_pair(values):
    inner_arg = ROOT_TWO_PI * (values + CUBIC * values * values * values)
    tangent = jnp.tanh(inner_arg)
    gelu_value = 0.5 * values * (1.0 + tangent)
    gelu_slope = 0.5 * (1.0 + tangent) + 0.5 * values * (1.0 - tangent * tangent) * ROOT_TWO_PI * (
        1.0 + 3.0 * CUBIC * values * values
    )
    return (gelu_value, gelu_slope)


def depthwise(padded, kernel):
    span = kernel.shape[0]
    rows, cols = padded.shape[0] - span + 1, padded.shape[1] - span + 1
    total = jnp.zeros((rows, cols, padded.shape[2]), jnp.float32)
    for down in range(span):
        for east in range(span):
            window = padded[down : down + rows, east : east + cols]
            total = total + window.astype(jnp.float32) * kernel[down, east]
    return total


def kernel_grads(back, framed, span):
    rows, cols = back.shape[:2]
    back_float = back.astype(jnp.float32)
    sums = []
    for down in range(span):
        for east in range(span):
            window = framed[down : down + rows, east : east + cols].astype(jnp.float32)
            sums.append(jnp.sum(back_float * window, axis=(0, 1)))
    return jnp.stack(sums)


def on_device(
    ocean_state,
    land_mask,
    cotangent,
    depth_kernel,
    norm_gain,
    norm_shift,
    weight_in,
    bias_in,
    weight_out,
    bias_out,
    layer_scale,
):
    devices = lax.axis_size("tiles")
    mine, core = lax.axis_index("tiles"), lax.axis_index("chan")
    slots = land_mask.shape[1]
    half = slots // 2
    side = ocean_state.shape[3]
    own = ocean_state.shape[4] // side
    chans = 2 * own
    span = depth_kernel.shape[0]
    margin = span // 2
    listed = cotangent.shape[0]
    width = half * side
    cells = side * width
    group = weight_in.shape[1]
    cap = -(-half // devices)

    masks = lax.all_gather(land_mask[0], "tiles")
    counts = jnp.sum(masks.reshape(2 * devices, half), axis=1)
    ends = jnp.cumsum(counts)
    starts = ends - counts
    home = mine * 2 + core
    my_start = starts[home]
    flags = lax.dynamic_slice(land_mask[0], (core * half,), (half,))
    inclusive = jnp.cumsum(flags)
    lap = jnp.arange(cap, dtype=jnp.int32)

    wanted = (mine - starts)[:, None] % devices + lap * devices
    wanted = jnp.clip((starts[:, None] + wanted) // devices, 0, listed - 1)
    leaving = jnp.take(cotangent[:, 0], wanted.reshape(-1), axis=0)
    landed = lax.all_to_all(leaving, ("tiles", "chan"), 0, 0, tiled=True)

    vectors = jnp.concatenate(
        [depth_kernel.reshape(-1), norm_gain, norm_shift, bias_out, layer_scale, bias_in]
    )
    others = swapped(vectors)

    def both(low, high, lead=()):
        return jnp.concatenate(
            [vectors[low:high].reshape(lead + (-1,)), others[low:high].reshape(lead + (-1,))],
            axis=-1,
        )

    taps = span * span * own
    kernel = both(0, taps, (span, span))
    gain = both(taps, taps + own)
    shift = both(taps + own, taps + 2 * own)
    bias_o = both(taps + 2 * own, taps + 3 * own)
    scale = both(taps + 3 * own, taps + 4 * own)
    bias_h = both(taps + 4 * own, taps + 4 * own + group)
    w_in = jnp.concatenate([weight_in, swapped(weight_in)], axis=1)
    w_in = jnp.where(core == 0, w_in, jnp.concatenate([w_in[own:], w_in[:own]], axis=0))
    w_out = jnp.concatenate([weight_out, swapped(weight_out)], axis=0)
    w_out = jnp.where(
        core == 0, w_out, jnp.concatenate([w_out[:, own:], w_out[:, :own]], axis=1)
    )

    state = ocean_state[0, :, 0].reshape(slots, side, side, own)
    masked = state * land_mask[0].astype(jnp.bfloat16)[:, None, None, None]
    field = masked.transpose(1, 0, 2, 3).reshape(side, slots * side, own)
    tall = row_halo(field, margin)
    tall = jnp.concatenate(
        [tall[:, slots * side - margin :], tall, tall[:, :margin]], axis=1
    )
    shape = (tall.shape[0], width + 2 * margin, own)
    kept = lax.dynamic_slice(tall, (0, core * width, 0), shape)
    given = lax.dynamic_slice(tall, (0, (1 - core) * width, 0), shape)
    framed = jnp.concatenate([kept, swapped(given)], axis=2)

    on_land = jnp.repeat(flags, side)[None, :, None] == 0
    mixed = jnp.where(on_land, 0.0, depthwise(framed, kernel)).reshape(cells, chans)
    cell_mean = jnp.sum(mixed, axis=1) / chans
    variance = jnp.sum(mixed * mixed, axis=1) / chans - cell_mean * cell_mean
    factor = lax.rsqrt(variance + EPS)
    normed = (mixed - cell_mean[:, None]) * factor[:, None]
    features = (normed * gain + shift).astype(jnp.bfloat16)
    hidden = jnp.dot(features, w_in, preferred_element_type=jnp.float32) + bias_h
    active, slope = gelu_pair(hidden)
    active = active.astype(jnp.bfloat16)
    branch = jnp.dot(active, w_out, preferred_element_type=jnp.float32) + bias_o
    residual = framed[margin : margin + side, margin : margin + width]
    residual = residual.astype(jnp.float32).reshape(cells, chans)
    block = (residual + scale * branch).astype(jnp.bfloat16)
    block = block.reshape(side, half, side, 2, own).transpose(1, 3, 0, 2, 4)
    block = block.reshape(half * 2, side, side * own)

    target = jnp.arange(devices, dtype=jnp.int32)
    rank = (target - my_start)[:, None] % devices + lap * devices
    source = jnp.sum((inclusive <= rank[..., None]).astype(jnp.int32), axis=-1)
    source = jnp.minimum(source, half - 1)
    part = (jnp.arange(2, dtype=jnp.int32) + core) % 2
    source = source[:, None, :] * 2 + part[None, :, None]
    leaving = jnp.take(block, source.reshape(-1), axis=0)
    finished = lax.all_to_all(leaving, ("tiles", "chan"), 0, 0, tiled=True)
    ranks = jnp.arange(listed, dtype=jnp.int32) * devices + mine
    owner = jnp.sum((ends[None, :] <= ranks[:, None]).astype(jnp.int32), axis=1)
    owner = jnp.minimum(owner, 2 * devices - 1)
    pick = owner * cap + (ranks - starts[owner]) // devices
    block_out = jnp.take(finished, pick, axis=0)[:, None]

    local = jnp.maximum(inclusive - 1, 0)
    pick = ((my_start + local) % devices)[:, None] * 2 + part
    pick = pick * cap + (local // devices)[:, None]
    upstream = jnp.take(landed, pick.reshape(-1), axis=0)
    upstream = upstream.reshape(half, 2, side, side, own).transpose(2, 0, 3, 1, 4)
    upstream = upstream.reshape(side, width, chans).astype(jnp.float32)
    upstream = jnp.where(on_land, 0.0, upstream).reshape(cells, chans)
    scaled = scale * upstream
    scaled_bf = scaled.astype(jnp.bfloat16)
    grad_scale = jnp.sum(upstream * branch, axis=0)
    grad_bias_out = jnp.sum(scaled, axis=0)
    grad_w_out = jnp.dot(active.T, scaled_bf, preferred_element_type=jnp.float32)
    back_hidden = jnp.dot(scaled_bf, w_out.T, preferred_element_type=jnp.float32) * slope
    back_hidden_bf = back_hidden.astype(jnp.bfloat16)
    grad_w_in = jnp.dot(features.T, back_hidden_bf, preferred_element_type=jnp.float32)
    grad_bias_in = jnp.sum(back_hidden, axis=0)
    back_features = jnp.dot(back_hidden_bf, w_in.T, preferred_element_type=jnp.float32)

    grad_w_in = jnp.where(
        core == 0, grad_w_in, jnp.concatenate([grad_w_in[own:], grad_w_in[:own]], axis=0)
    )
    grad_w_out = jnp.where(
        core == 0,
        grad_w_out,
        jnp.concatenate([grad_w_out[:, own:], grad_w_out[:, :own]], axis=1),
    )
    norm_cells = float(devices * listed * side * side) ** 0.5
    grad_w_in = (grad_w_in[:, :group] + swapped(grad_w_in[:, group:])) / norm_cells
    grad_w_out = (grad_w_out[:group] + swapped(grad_w_out[group:])) / norm_cells
    grad_w_in, grad_w_out = lax.psum((grad_w_in, grad_w_out), "tiles")

    back_normed = back_features * gain
    grad_gain = jnp.sum(back_features * normed, axis=0)
    grad_shift = jnp.sum(back_features, axis=0)
    first = jnp.sum(back_normed, axis=1) / chans
    second = jnp.sum(back_normed * normed, axis=1) / chans
    back_mixed = factor[:, None] * (back_normed - first[:, None] - normed * second[:, None])
    back = back_mixed.astype(jnp.bfloat16).reshape(side, width, chans)

    back_tall = row_halo(back, margin)
    rims = swapped(
        jnp.concatenate([back_tall[:, :margin], back_tall[:, width - margin :]], axis=1)
    )
    rims = jnp.concatenate([rims[..., own:], rims[..., :own]], axis=2)
    back_framed = jnp.concatenate([rims[:, margin:], back_tall, rims[:, :margin]], axis=1)
    grad_field = depthwise(back_framed, kernel[::-1, ::-1])
    grad_field = jnp.where(on_land, 0.0, grad_field).astype(jnp.bfloat16)
    grad_kept, grad_got = grad_field[..., :own], swapped(grad_field[..., own:])
    grad_cells = jnp.where(
        core == 0,
        jnp.concatenate([grad_kept, grad_got], axis=1),
        jnp.concatenate([grad_got, grad_kept], axis=1),
    )
    grad_cells = grad_cells.reshape(side, slots, side, own).transpose(1, 0, 2, 3)
    grad_state = grad_cells.reshape(1, slots, 1, side, side * own)

    grad_kernel = kernel_grads(back, framed, span)
    by_channel = jnp.concatenate(
        [grad_kernel, jnp.stack([grad_gain, grad_shift, grad_bias_out, grad_scale])], axis=0
    )
    keep = jnp.concatenate([by_channel[:, :own].reshape(-1), grad_bias_in[:group]])
    give = jnp.concatenate([by_channel[:, own:].reshape(-1), grad_bias_in[group:]])
    summed = lax.psum(keep + swapped(give), "tiles") / norm_cells
    ends_at = span * span * own
    rows = summed[ends_at : ends_at + 4 * own].reshape(4, own)
    return (
        block_out,
        grad_state,
        summed[:ends_at].reshape(span, span, own),
        rows[0],
        rows[1],
        grad_w_in,
        summed[ends_at + 4 * own :],
        grad_w_out,
        rows[2],
        rows[3],
    )


def solution(mesh):
    in_specs = (
        P("tiles", None, "chan", None, None),
        P("tiles", None),
        P("tiles", "chan", None, None),
        P(None, None, "chan"),
        P("chan"),
        P("chan"),
        P(None, "chan"),
        P("chan"),
        P("chan", None),
        P("chan"),
        P("chan"),
    )
    out_specs = (
        P("tiles", "chan", None, None),
        P("tiles", None, "chan", None, None),
        P(None, None, "chan"),
        P("chan"),
        P("chan"),
        P(None, "chan"),
        P("chan"),
        P("chan", None),
        P("chan"),
        P("chan"),
    )
    return jax.shard_map(
        on_device, mesh=mesh, in_specs=in_specs, out_specs=out_specs, check_vma=False
    )
```

```python
import jax
import jax.numpy as jnp
from jax import lax
from jax.sharding import PartitionSpec as P

EPS = 1e-06
ROOT_TWO_PI = 0.7978845608028654
CUBIC = 0.044715
SWAP = ((0, 1), (1, 0))


def swapped(value):
    return lax.ppermute(value, "chan", SWAP)


def row_halo(field, width):
    count = lax.axis_size("tiles")
    forward = [(i, i + 1) for i in range(count - 1)]
    backward = [(target, source) for source, target in forward]
    low = lax.ppermute(field[field.shape[0] - width :], "tiles", forward)
    high = lax.ppermute(field[:width], "tiles", backward)
    return jnp.concatenate([low, field, high], axis=0)


def gelu_pair(values):
    inner_arg = ROOT_TWO_PI * (values + CUBIC * values * values * values)
    tangent = jnp.tanh(inner_arg)
    gelu_value = 0.5 * values * (1.0 + tangent)
    gelu_slope = 0.5 * (1.0 + tangent) + 0.5 * values * (1.0 - tangent * tangent) * ROOT_TWO_PI * (
        1.0 + 3.0 * CUBIC * values * values
    )
    return (gelu_value, gelu_slope)


def strips(field, count):
    rows, cols, chans = field.shape
    return field.reshape(rows, count, cols // count, chans).transpose(0, 2, 1, 3)


def unstrip(value):
    rows, cols, count, chans = value.shape
    return value.transpose(0, 2, 1, 3).reshape(rows, count * cols, chans)


def framed_strips(padded, count, reach):
    width = padded.shape[1] - reach
    body = strips(padded[:, :width], count)
    last = padded[:, width:][:, :, None]
    tail = jnp.concatenate([body[:, :reach, 1:], last], axis=2)
    return jnp.concatenate([body, tail], axis=1)


def depthwise(padded, kernel):
    span = kernel.shape[0]
    rows, cols = padded.shape[0] - span + 1, padded.shape[1] - span + 1
    total = jnp.zeros((rows, cols) + padded.shape[2:], jnp.float32)
    for down in range(span):
        for east in range(span):
            window = padded[down : down + rows, east : east + cols]
            total = total + window.astype(jnp.float32) * kernel[down, east]
    return total


def kernel_grads(back, framed, span):
    rows, cols = back.shape[:2]
    back_float = back.astype(jnp.float32)
    sums = []
    for down in range(span):
        for east in range(span):
            window = framed[down : down + rows, east : east + cols].astype(jnp.float32)
            sums.append(jnp.sum(back_float * window, axis=(0, 1, 2)))
    return jnp.stack(sums)


def on_device(
    ocean_state,
    land_mask,
    cotangent,
    depth_kernel,
    norm_gain,
    norm_shift,
    weight_in,
    bias_in,
    weight_out,
    bias_out,
    layer_scale,
):
    devices = lax.axis_size("tiles")
    mine, core = lax.axis_index("tiles"), lax.axis_index("chan")
    slots = land_mask.shape[1]
    half = slots // 2
    side = ocean_state.shape[3]
    own = ocean_state.shape[4] // side
    chans = 2 * own
    span = depth_kernel.shape[0]
    margin = span // 2
    listed = cotangent.shape[0]
    width = half * side
    cells = side * width
    group = weight_in.shape[1]
    cap = -(-half // devices)

    masks = lax.all_gather(land_mask[0], "tiles")
    counts = jnp.sum(masks.reshape(2 * devices, half), axis=1)
    ends = jnp.cumsum(counts)
    starts = ends - counts
    home = mine * 2 + core
    my_start = starts[home]
    flags = lax.dynamic_slice(land_mask[0], (core * half,), (half,))
    inclusive = jnp.cumsum(flags)
    lap = jnp.arange(cap, dtype=jnp.int32)

    wanted = (mine - starts)[:, None] % devices + lap * devices
    wanted = jnp.clip((starts[:, None] + wanted) // devices, 0, listed - 1)
    leaving = jnp.take(cotangent[:, 0], wanted.reshape(-1), axis=0)
    landed = lax.all_to_all(leaving, ("tiles", "chan"), 0, 0, tiled=True)

    vectors = jnp.concatenate(
        [depth_kernel.reshape(-1), norm_gain, norm_shift, bias_out, layer_scale, bias_in]
    )
    others = swapped(vectors)

    def both(low, high, lead=()):
        return jnp.concatenate(
            [vectors[low:high].reshape(lead + (-1,)), others[low:high].reshape(lead + (-1,))],
            axis=-1,
        )

    taps = span * span * own
    kernel = both(0, taps, (span, span))
    gain = both(taps, taps + own)
    shift = both(taps + own, taps + 2 * own)
    bias_o = both(taps + 2 * own, taps + 3 * own)
    scale = both(taps + 3 * own, taps + 4 * own)
    bias_h = both(taps + 4 * own, taps + 4 * own + group)
    w_in = jnp.concatenate([weight_in, swapped(weight_in)], axis=1)
    w_in = jnp.where(core == 0, w_in, jnp.concatenate([w_in[own:], w_in[:own]], axis=0))
    w_out = jnp.concatenate([weight_out, swapped(weight_out)], axis=0)
    w_out = jnp.where(
        core == 0, w_out, jnp.concatenate([w_out[:, own:], w_out[:, :own]], axis=1)
    )

    state = ocean_state[0, :, 0].reshape(slots, side, side, own)
    masked = state * land_mask[0].astype(jnp.bfloat16)[:, None, None, None]
    field = masked.transpose(1, 0, 2, 3).reshape(side, slots * side, own)
    tall = row_halo(field, margin)
    tall = jnp.concatenate(
        [tall[:, slots * side - margin :], tall, tall[:, :margin]], axis=1
    )
    shape = (tall.shape[0], width + 2 * margin, own)
    kept = lax.dynamic_slice(tall, (0, core * width, 0), shape)
    given = lax.dynamic_slice(tall, (0, (1 - core) * width, 0), shape)
    framed = jnp.concatenate([kept, swapped(given)], axis=2)
    framed = framed_strips(framed, side, 2 * margin)

    on_land = strips(jnp.repeat(flags, side)[None, :, None], side) == 0
    mixed = jnp.where(on_land, 0.0, depthwise(framed, kernel)).reshape(cells, chans)
    cell_mean = jnp.sum(mixed, axis=1) / chans
    variance = jnp.sum(mixed * mixed, axis=1) / chans - cell_mean * cell_mean
    factor = lax.rsqrt(variance + EPS)
    normed = (mixed - cell_mean[:, None]) * factor[:, None]
    features = (normed * gain + shift).astype(jnp.bfloat16)
    hidden = jnp.dot(features, w_in, preferred_element_type=jnp.float32) + bias_h
    active, slope = gelu_pair(hidden)
    active = active.astype(jnp.bfloat16)
    branch = jnp.dot(active, w_out, preferred_element_type=jnp.float32) + bias_o
    residual = framed[margin : margin + side, margin : margin + half]
    residual = residual.astype(jnp.float32).reshape(cells, chans)
    block = (residual + scale * branch).astype(jnp.bfloat16)
    block = unstrip(block.reshape(side, half, side, chans)).reshape(side, half, side, 2, own).transpose(1, 3, 0, 2, 4)
    block = block.reshape(half * 2, side, side * own)

    target = jnp.arange(devices, dtype=jnp.int32)
    rank = (target - my_start)[:, None] % devices + lap * devices
    source = jnp.sum((inclusive <= rank[..., None]).astype(jnp.int32), axis=-1)
    source = jnp.minimum(source, half - 1)
    part = (jnp.arange(2, dtype=jnp.int32) + core) % 2
    source = source[:, None, :] * 2 + part[None, :, None]
    leaving = jnp.take(block, source.reshape(-1), axis=0)
    finished = lax.all_to_all(leaving, ("tiles", "chan"), 0, 0, tiled=True)
    ranks = jnp.arange(listed, dtype=jnp.int32) * devices + mine
    owner = jnp.sum((ends[None, :] <= ranks[:, None]).astype(jnp.int32), axis=1)
    owner = jnp.minimum(owner, 2 * devices - 1)
    pick = owner * cap + (ranks - starts[owner]) // devices
    block_out = jnp.take(finished, pick, axis=0)[:, None]

    local = jnp.maximum(inclusive - 1, 0)
    pick = ((my_start + local) % devices)[:, None] * 2 + part
    pick = pick * cap + (local // devices)[:, None]
    upstream = jnp.take(landed, pick.reshape(-1), axis=0)
    upstream = upstream.reshape(half, 2, side, side, own).transpose(2, 0, 3, 1, 4)
    upstream = strips(upstream.reshape(side, width, chans), side).astype(jnp.float32)
    upstream = jnp.where(on_land, 0.0, upstream).reshape(cells, chans)
    scaled = scale * upstream
    scaled_bf = scaled.astype(jnp.bfloat16)
    grad_scale = jnp.sum(upstream * branch, axis=0)
    grad_bias_out = jnp.sum(scaled, axis=0)
    grad_w_out = jnp.dot(active.T, scaled_bf, preferred_element_type=jnp.float32)
    back_hidden = jnp.dot(scaled_bf, w_out.T, preferred_element_type=jnp.float32) * slope
    back_hidden_bf = back_hidden.astype(jnp.bfloat16)
    grad_w_in = jnp.dot(features.T, back_hidden_bf, preferred_element_type=jnp.float32)
    grad_bias_in = jnp.sum(back_hidden, axis=0)
    back_features = jnp.dot(back_hidden_bf, w_in.T, preferred_element_type=jnp.float32)

    grad_w_in = jnp.where(
        core == 0, grad_w_in, jnp.concatenate([grad_w_in[own:], grad_w_in[:own]], axis=0)
    )
    grad_w_out = jnp.where(
        core == 0,
        grad_w_out,
        jnp.concatenate([grad_w_out[:, own:], grad_w_out[:, :own]], axis=1),
    )
    norm_cells = float(devices * listed * side * side) ** 0.5
    grad_w_in = (grad_w_in[:, :group] + swapped(grad_w_in[:, group:])) / norm_cells
    grad_w_out = (grad_w_out[:group] + swapped(grad_w_out[group:])) / norm_cells

    back_normed = back_features * gain
    grad_gain = jnp.sum(back_features * normed, axis=0)
    grad_shift = jnp.sum(back_features, axis=0)
    first = jnp.sum(back_normed, axis=1) / chans
    second = jnp.sum(back_normed * normed, axis=1) / chans
    back_mixed = factor[:, None] * (back_normed - first[:, None] - normed * second[:, None])
    back = back_mixed.astype(jnp.bfloat16).reshape(side, half, side, chans)

    back_tall = row_halo(unstrip(back), margin)
    rims = swapped(
        jnp.concatenate([back_tall[:, :margin], back_tall[:, width - margin :]], axis=1)
    )
    rims = jnp.concatenate([rims[..., own:], rims[..., :own]], axis=2)
    back_framed = jnp.concatenate([rims[:, margin:], back_tall, rims[:, :margin]], axis=1)
    grad_field = depthwise(framed_strips(back_framed, side, 2 * margin), kernel[::-1, ::-1])
    grad_field = unstrip(jnp.where(on_land, 0.0, grad_field).astype(jnp.bfloat16))
    grad_kept, grad_got = grad_field[..., :own], swapped(grad_field[..., own:])
    grad_cells = jnp.where(
        core == 0,
        jnp.concatenate([grad_kept, grad_got], axis=1),
        jnp.concatenate([grad_got, grad_kept], axis=1),
    )
    grad_cells = grad_cells.reshape(side, slots, side, own).transpose(1, 0, 2, 3)
    grad_state = grad_cells.reshape(1, slots, 1, side, side * own)

    grad_kernel = kernel_grads(back, framed, span)
    by_channel = jnp.concatenate(
        [grad_kernel, jnp.stack([grad_gain, grad_shift, grad_bias_out, grad_scale])], axis=0
    )
    keep = jnp.concatenate([by_channel[:, :own].reshape(-1), grad_bias_in[:group]])
    give = jnp.concatenate([by_channel[:, own:].reshape(-1), grad_bias_in[group:]])
    small = (keep + swapped(give)) / norm_cells
    lines = -(-small.shape[0] // chans)
    small = jnp.pad(small, (0, lines * chans - small.shape[0])).reshape(lines, chans)
    together = jnp.concatenate([grad_w_out, grad_w_in.reshape(group, chans), small], axis=0)
    together = lax.psum(together, "tiles")
    grad_w_out = together[:group]
    grad_w_in = together[group : 2 * group].reshape(chans, group)
    summed = together[2 * group :].reshape(-1)
    ends_at = span * span * own
    rows = summed[ends_at : ends_at + 4 * own].reshape(4, own)
    return (
        block_out,
        grad_state,
        summed[:ends_at].reshape(span, span, own),
        rows[0],
        rows[1],
        grad_w_in,
        summed[ends_at + 4 * own : ends_at + 4 * own + group],
        grad_w_out,
        rows[2],
        rows[3],
    )


def solution(mesh):
    in_specs = (
        P("tiles", None, "chan", None, None),
        P("tiles", None),
        P("tiles", "chan", None, None),
        P(None, None, "chan"),
        P("chan"),
        P("chan"),
        P(None, "chan"),
        P("chan"),
        P("chan", None),
        P("chan"),
        P("chan"),
    )
    out_specs = (
        P("tiles", "chan", None, None),
        P("tiles", None, "chan", None, None),
        P(None, None, "chan"),
        P("chan"),
        P("chan"),
        P(None, "chan"),
        P("chan"),
        P("chan", None),
        P("chan"),
        P("chan"),
    )
    return jax.shard_map(
        on_device, mesh=mesh, in_specs=in_specs, out_specs=out_specs, check_vma=False
    )
```

```python
import jax
import jax.numpy as jnp
from jax import lax
from jax.sharding import PartitionSpec as P

EPS = 1e-06
ROOT_TWO_PI = 0.7978845608028654
CUBIC = 0.044715
SWAP = ((0, 1), (1, 0))


def swapped(value):
    return lax.ppermute(value, "chan", SWAP)


def row_halo(field, width):
    count = lax.axis_size("tiles")
    forward = [(i, i + 1) for i in range(count - 1)]
    backward = [(target, source) for source, target in forward]
    low = lax.ppermute(field[field.shape[0] - width :], "tiles", forward)
    high = lax.ppermute(field[:width], "tiles", backward)
    return jnp.concatenate([low, field, high], axis=0)


def gelu_pair(values):
    inner_arg = ROOT_TWO_PI * (values + CUBIC * values * values * values)
    tangent = jnp.tanh(inner_arg)
    gelu_value = 0.5 * values * (1.0 + tangent)
    gelu_slope = 0.5 * (1.0 + tangent) + 0.5 * values * (1.0 - tangent * tangent) * ROOT_TWO_PI * (
        1.0 + 3.0 * CUBIC * values * values
    )
    return (gelu_value, gelu_slope)


def strips(field, count):
    rows, cols, chans = field.shape
    return field.reshape(rows, count, cols // count, chans).transpose(0, 2, 1, 3)


def unstrip(value):
    rows, cols, count, chans = value.shape
    return value.transpose(0, 2, 1, 3).reshape(rows, count * cols, chans)


def framed_strips(padded, count, reach):
    width = padded.shape[1] - reach
    body = strips(padded[:, :width], count)
    last = padded[:, width:][:, :, None]
    tail = jnp.concatenate([body[:, :reach, 1:], last], axis=2)
    return jnp.concatenate([body, tail], axis=1)


def depthwise(padded, kernel):
    span = kernel.shape[0]
    rows, cols = padded.shape[0] - span + 1, padded.shape[1] - span + 1
    total = jnp.zeros((rows, cols) + padded.shape[2:], jnp.float32)
    for down in range(span):
        for east in range(span):
            window = padded[down : down + rows, east : east + cols]
            total = total + window.astype(jnp.float32) * kernel[down, east]
    return total


def kernel_grads(back, framed, span):
    rows, cols = back.shape[:2]
    back_float = back.astype(jnp.float32)
    sums = []
    for down in range(span):
        for east in range(span):
            window = framed[down : down + rows, east : east + cols].astype(jnp.float32)
            sums.append(jnp.sum(back_float * window, axis=(0, 1, 2)))
    return jnp.stack(sums)


def on_device(
    ocean_state,
    land_mask,
    cotangent,
    depth_kernel,
    norm_gain,
    norm_shift,
    weight_in,
    bias_in,
    weight_out,
    bias_out,
    layer_scale,
):
    devices = lax.axis_size("tiles")
    mine, core = lax.axis_index("tiles"), lax.axis_index("chan")
    slots = land_mask.shape[1]
    half = slots // 2
    side = ocean_state.shape[3]
    own = ocean_state.shape[4] // side
    chans = 2 * own
    span = depth_kernel.shape[0]
    margin = span // 2
    listed = cotangent.shape[0]
    width = half * side
    cells = side * width
    group = weight_in.shape[1]
    cap = -(-half // devices)

    masks = lax.all_gather(land_mask[0], "tiles")
    counts = jnp.sum(masks.reshape(2 * devices, half), axis=1)
    ends = jnp.cumsum(counts)
    starts = ends - counts
    home = mine * 2 + core
    my_start = starts[home]
    flags = lax.dynamic_slice(land_mask[0], (core * half,), (half,))
    inclusive = jnp.cumsum(flags)
    lap = jnp.arange(cap, dtype=jnp.int32)

    wanted = (mine - starts)[:, None] % devices + lap * devices
    wanted = jnp.clip((starts[:, None] + wanted) // devices, 0, listed - 1)
    leaving = jnp.take(cotangent[:, 0], wanted.reshape(-1), axis=0)
    landed = lax.all_to_all(leaving, ("tiles", "chan"), 0, 0, tiled=True)

    vectors = jnp.concatenate(
        [depth_kernel.reshape(-1), norm_gain, norm_shift, bias_out, layer_scale, bias_in]
    )
    others = swapped(vectors)

    def both(low, high, lead=()):
        return jnp.concatenate(
            [vectors[low:high].reshape(lead + (-1,)), others[low:high].reshape(lead + (-1,))],
            axis=-1,
        )

    taps = span * span * own
    kernel = both(0, taps, (span, span))
    gain = both(taps, taps + own)
    shift = both(taps + own, taps + 2 * own)
    bias_o = both(taps + 2 * own, taps + 3 * own)
    scale = both(taps + 3 * own, taps + 4 * own)
    bias_h = both(taps + 4 * own, taps + 4 * own + group)
    w_in = jnp.concatenate([weight_in, swapped(weight_in)], axis=1)
    w_in = jnp.where(core == 0, w_in, jnp.concatenate([w_in[own:], w_in[:own]], axis=0))
    w_out = jnp.concatenate([weight_out, swapped(weight_out)], axis=0)
    w_out = jnp.where(
        core == 0, w_out, jnp.concatenate([w_out[:, own:], w_out[:, :own]], axis=1)
    )

    state = ocean_state[0, :, 0].reshape(slots, side, side, own)
    masked = state * land_mask[0].astype(jnp.bfloat16)[:, None, None, None]
    field = masked.transpose(1, 0, 2, 3).reshape(side, slots * side, own)
    tall = row_halo(field, margin)
    tall = jnp.concatenate(
        [tall[:, slots * side - margin :], tall, tall[:, :margin]], axis=1
    )
    shape = (tall.shape[0], width + 2 * margin, own)
    kept = lax.dynamic_slice(tall, (0, core * width, 0), shape)
    given = lax.dynamic_slice(tall, (0, (1 - core) * width, 0), shape)
    framed = jnp.concatenate([kept, swapped(given)], axis=2)
    framed = framed_strips(framed, side, 2 * margin)

    on_land = strips(jnp.repeat(flags, side)[None, :, None], side) == 0
    mixed = jnp.where(on_land, 0.0, depthwise(framed, kernel)).reshape(cells, chans)
    cell_mean = jnp.sum(mixed, axis=1) / chans
    variance = jnp.sum(mixed * mixed, axis=1) / chans - cell_mean * cell_mean
    factor = lax.rsqrt(variance + EPS)
    normed = (mixed - cell_mean[:, None]) * factor[:, None]
    features = (normed * gain + shift).astype(jnp.bfloat16)
    hidden = jnp.dot(features, w_in, preferred_element_type=jnp.float32) + bias_h
    active, slope = gelu_pair(hidden)
    active = active.astype(jnp.bfloat16)
    branch = jnp.dot(active, w_out, preferred_element_type=jnp.float32) + bias_o
    residual = framed[margin : margin + side, margin : margin + half]
    residual = residual.astype(jnp.float32).reshape(cells, chans)
    block = (residual + scale * branch).astype(jnp.bfloat16)
    block = unstrip(block.reshape(side, half, side, chans)).reshape(side, half, side, 2, own).transpose(1, 3, 0, 2, 4)
    block = block.reshape(half * 2, side, side * own)

    target = jnp.arange(devices, dtype=jnp.int32)
    rank = (target - my_start)[:, None] % devices + lap * devices
    source = jnp.sum((inclusive <= rank[..., None]).astype(jnp.int32), axis=-1)
    source = jnp.minimum(source, half - 1)
    part = (jnp.arange(2, dtype=jnp.int32) + core) % 2
    source = source[:, None, :] * 2 + part[None, :, None]
    leaving = jnp.take(block, source.reshape(-1), axis=0)
    finished = lax.all_to_all(leaving, ("tiles", "chan"), 0, 0, tiled=True)
    ranks = jnp.arange(listed, dtype=jnp.int32) * devices + mine
    owner = jnp.sum((ends[None, :] <= ranks[:, None]).astype(jnp.int32), axis=1)
    owner = jnp.minimum(owner, 2 * devices - 1)
    pick = owner * cap + (ranks - starts[owner]) // devices
    block_out = jnp.take(finished, pick, axis=0)[:, None]

    local = jnp.maximum(inclusive - 1, 0)
    pick = ((my_start + local) % devices)[:, None] * 2 + part
    pick = pick * cap + (local // devices)[:, None]
    upstream = jnp.take(landed, pick.reshape(-1), axis=0)
    upstream = upstream.reshape(half, 2, side, side, own).transpose(2, 0, 3, 1, 4)
    upstream = strips(upstream.reshape(side, width, chans), side).astype(jnp.float32)
    upstream = jnp.where(on_land, 0.0, upstream).reshape(cells, chans)
    scaled = scale * upstream
    scaled_bf = scaled.astype(jnp.bfloat16)
    grad_scale = jnp.sum(upstream * branch, axis=0)
    grad_bias_out = jnp.sum(scaled, axis=0)
    grad_w_out = jnp.dot(active.T, scaled_bf, preferred_element_type=jnp.float32)
    back_hidden = jnp.dot(scaled_bf, w_out.T, preferred_element_type=jnp.float32) * slope
    back_hidden_bf = back_hidden.astype(jnp.bfloat16)
    grad_w_in = jnp.dot(features.T, back_hidden_bf, preferred_element_type=jnp.float32)
    grad_bias_in = jnp.sum(back_hidden, axis=0)
    back_features = jnp.dot(back_hidden_bf, w_in.T, preferred_element_type=jnp.float32)

    grad_w_in = jnp.where(
        core == 0, grad_w_in, jnp.concatenate([grad_w_in[own:], grad_w_in[:own]], axis=0)
    )
    grad_w_out = jnp.where(
        core == 0,
        grad_w_out,
        jnp.concatenate([grad_w_out[:, own:], grad_w_out[:, :own]], axis=1),
    )
    norm_cells = float(devices * listed * side * side) ** 0.5
    grad_w_in = (grad_w_in[:, :group] + swapped(grad_w_in[:, group:])) / norm_cells
    grad_w_out = (grad_w_out[:group] + swapped(grad_w_out[group:])) / norm_cells

    back_normed = back_features * gain
    grad_gain = jnp.sum(back_features * normed, axis=0)
    grad_shift = jnp.sum(back_features, axis=0)
    first = jnp.sum(back_normed, axis=1) / chans
    second = jnp.sum(back_normed * normed, axis=1) / chans
    back_mixed = factor[:, None] * (back_normed - first[:, None] - normed * second[:, None])
    back = back_mixed.astype(jnp.bfloat16).reshape(side, half, side, chans)

    back_tall = row_halo(unstrip(back), margin)
    rims = swapped(
        jnp.concatenate([back_tall[:, :margin], back_tall[:, width - margin :]], axis=1)
    )
    rims = jnp.concatenate([rims[..., own:], rims[..., :own]], axis=2)
    back_framed = jnp.concatenate([rims[:, margin:], back_tall, rims[:, :margin]], axis=1)
    grad_field = depthwise(back_framed, kernel[::-1, ::-1])
    land_cols = jnp.repeat(flags, side)[None, :, None] == 0
    grad_field = jnp.where(land_cols, 0.0, grad_field).astype(jnp.bfloat16)
    grad_kept, grad_got = grad_field[..., :own], swapped(grad_field[..., own:])
    grad_cells = jnp.where(
        core == 0,
        jnp.concatenate([grad_kept, grad_got], axis=1),
        jnp.concatenate([grad_got, grad_kept], axis=1),
    )
    grad_cells = grad_cells.reshape(side, slots, side, own).transpose(1, 0, 2, 3)
    grad_state = grad_cells.reshape(1, slots, 1, side, side * own)

    grad_kernel = kernel_grads(back, framed, span)
    by_channel = jnp.concatenate(
        [grad_kernel, jnp.stack([grad_gain, grad_shift, grad_bias_out, grad_scale])], axis=0
    )
    keep = jnp.concatenate([by_channel[:, :own].reshape(-1), grad_bias_in[:group]])
    give = jnp.concatenate([by_channel[:, own:].reshape(-1), grad_bias_in[group:]])
    small = (keep + swapped(give)) / norm_cells
    lines = -(-small.shape[0] // chans)
    small = jnp.pad(small, (0, lines * chans - small.shape[0])).reshape(lines, chans)
    together = jnp.concatenate([grad_w_out, grad_w_in.reshape(group, chans), small], axis=0)
    together = lax.psum(together, "tiles")
    grad_w_out = together[:group]
    grad_w_in = together[group : 2 * group].reshape(chans, group)
    summed = together[2 * group :].reshape(-1)
    ends_at = span * span * own
    rows = summed[ends_at : ends_at + 4 * own].reshape(4, own)
    return (
        block_out,
        grad_state,
        summed[:ends_at].reshape(span, span, own),
        rows[0],
        rows[1],
        grad_w_in,
        summed[ends_at + 4 * own : ends_at + 4 * own + group],
        grad_w_out,
        rows[2],
        rows[3],
    )


def solution(mesh):
    in_specs = (
        P("tiles", None, "chan", None, None),
        P("tiles", None),
        P("tiles", "chan", None, None),
        P(None, None, "chan"),
        P("chan"),
        P("chan"),
        P(None, "chan"),
        P("chan"),
        P("chan", None),
        P("chan"),
        P("chan"),
    )
    out_specs = (
        P("tiles", "chan", None, None),
        P("tiles", None, "chan", None, None),
        P(None, None, "chan"),
        P("chan"),
        P("chan"),
        P(None, "chan"),
        P("chan"),
        P("chan", None),
        P("chan"),
        P("chan"),
    )
    return jax.shard_map(
        on_device, mesh=mesh, in_specs=in_specs, out_specs=out_specs, check_vma=False
    )
```
